32 devices in a mesh: rep: 2 (over x), ep: 16 (over z, y, core).
Axes of the slice: x: 2, y: 2, z: 4, core: 2. Of those that a mesh axis runs over, the one named last changes fastest.
Arguments:
- tokens: bfloat16 [4096, 1024], P(('rep', 'ep')), may hold values from -6 to 6
- query: bfloat16 [4096, 1024], P(('rep', 'ep')), may hold values from -6 to 6
- expert_ids: int32 [4096, 6], P(('rep', 'ep')), may hold values from 0 to 15, all different within a row; in each aligned block of 128 rows (0 to 127, 128 to 255, ...) at most 49 rows name the same one
- gate_probs: bfloat16 [4096, 6], P(('rep', 'ep')), may hold values from 0.049804688 to 0.34960938
- w_gate_up: bfloat16 [16, 1024, 1408], P('ep'), may hold values from -0.1875 to 0.1875
- w_down: bfloat16 [16, 1024, 704], P('ep', 'rep'), may hold values from -0.1875 to 0.1875
- dir_gate: bfloat16 [16, 1024, 704], P('ep', 'rep'), may hold values from -0.1875 to 0.1875
Outputs:
- hvp_gate_up: float32 [16, 1024, 1408], P('ep', 'rep')
The draws below stay inside these ranges and needn't reach their ends.
Inputs may be any that keep to these rules, and one draw needn't show every extreme that they name: `expert_ids`: each row names 6 different experts; among the rows of one device no expert is named by more than 49 pairs, and in every draw some expert is named by exactly 49 pairs of some device.
All inputs are finite; a program needn't handle non-finite values.
Results may differ from the reference program's by a relative error of at most 0.015.
Values may be sent and summed in bfloat16 or wider, within the bound.
A program may use at most 64 MiB of HBM per device.

```python
import math
import jax
import jax.numpy as jnp
import numpy as np
from jax import lax

D = 1024
FF = 704
TOPK = 6
TOK_DEV = 128
EXPERTS = 16
CAP = 49
TOK_REP = 2048
TOKENS = 4096
N_REP = 2
N_EP = 16


def levels(stream_key, shape, pieces, smallest, largest):
    level, own = 1.0, jax.random.fold_in(stream_key, 6)
    for axis_at, blocks in pieces:
        steps = jnp.exp(jax.random.uniform(jax.random.fold_in(own, axis_at), (blocks,), jnp.float32, smallest / len(pieces), largest / len(pieces)))
        level = level * jnp.repeat(steps, shape[axis_at] // blocks).reshape([-1 if axis == axis_at else 1 for axis in range(len(shape))])
    return level


def deal_out(rng, own, number, rows, amount, top, reach, skew):
    order = jax.random.permutation(rng, amount)
    crowded, ordinary = shares(amount, rows * top, reach, skew, True), shares(amount, rows * top, reach, skew, False)
    places = jnp.arange(amount)

    def named(lengths, offset_by):
        used = int((lengths > 0).sum())
        fixed = max(1, used // 4)
        moved = fixed + (places - fixed + offset_by * (used - fixed)) % max(1, amount - fixed)
        return jnp.zeros((amount,), jnp.int32).at[order[jnp.where(places < fixed, places, moved)]].set(jnp.asarray(lengths, jnp.int32))

    lengths = jnp.where(number % 4 == 0, named(crowded, number // 4), named(ordinary, number - number // 4 - 1))
    mixed = jax.random.permutation(jax.random.fold_in(own, 3), amount)
    source_of, sink = mixed[0:amount // 2 * 2:2], mixed[1:amount // 2 * 2:2]
    slack = jnp.minimum(lengths[source_of] - 1, reach - lengths[sink]) // 2
    slack = jnp.where((source_of == order[0]) | (sink == order[0]) | (lengths[sink] == 0), 0, jnp.maximum(slack, 0))
    moved = jax.random.randint(jax.random.fold_in(own, 4), (amount // 2,), 0, 1 << 20) % (slack + 1)
    lengths = lengths.at[source_of].add(-moved).at[sink].add(moved)
    items = jnp.searchsorted(jnp.cumsum(lengths), jnp.arange(rows * top), side="right").astype(jnp.int32)
    listing = items.reshape(top, rows).T
    listing = listing[jax.random.permutation(jax.random.fold_in(own, 1), rows)]
    offset_by = jax.random.randint(jax.random.fold_in(own, 2), (rows, 1), 0, top)
    return jnp.take_along_axis(listing, (jnp.arange(top)[None, :] + offset_by) % top, axis=1)


def shares(count, total, most, skew, full):
    loads = [(1 << 20) // math.isqrt(standing ** skew) + 1 for standing in range(1, count + 1)]
    largest = most if full else min(most, max(-(-total // count), total * loads[0] // sum(loads)))
    least = 1 if total - largest >= count - 1 else 0
    counts, spare = [largest] + [least] * (count - 1), total - largest - least * (count - 1)
    while spare > 0:
        movable = [i for i in range(1, count) if counts[i] < largest] or [i for i in range(1, count) if counts[i] < most]
        pool, remaining = sum([loads[i] for i in movable]), spare
        for i in movable:
            extra = min(most - counts[i], max(1, remaining * loads[i] // pool), spare)
            counts[i] = counts[i] + extra
            spare = spare - extra
    return np.array(counts)


def gaussian(key, shape, width, reach, split=(), kind=jnp.bfloat16):
    level = levels(key, shape, split, -0.22, 0.18) if split else 1.0
    result = jax.random.normal(key, shape, jnp.float32) * width * level
    return jnp.minimum(jnp.maximum(result, -reach), reach).astype(kind)


def setup_inputs(seed: int = 0) -> dict:
    arg_keys = jax.random.split(jax.random.key(seed), 8)
    tokens = gaussian(arg_keys[0], (TOKENS, D), 1.0, 6.0, ((0, 32),))
    query = gaussian(arg_keys[1], (TOKENS, D), 1.0, 6.0, ((0, 32),))
    expert_ids_keys = jax.random.split(jax.random.fold_in(arg_keys[2], 1), TOKENS // TOK_DEV)
    expert_ids_turns = jax.random.permutation(jax.random.fold_in(arg_keys[2], 3), TOKENS // TOK_DEV)
    expert_ids = jax.vmap(lambda own, number: deal_out(jax.random.fold_in(arg_keys[2], 2), own, number, TOK_DEV, EXPERTS, TOPK, CAP, 2))(expert_ids_keys, expert_ids_turns).reshape((TOKENS, TOPK))
    gate_probs = jnp.clip(0.049804688 + 0.2998047 * jax.random.uniform(arg_keys[3], (TOKENS, TOPK), jnp.float32) ** levels(arg_keys[3], (TOKENS, TOPK), ((0, 32),), -0.2, 0.2), 0.049804688, 0.34960938).astype(jnp.bfloat16)
    w_gate_up = gaussian(arg_keys[4], (EXPERTS, D, 2 * FF), D ** -0.5, 0.1875, ((0, 16),))
    w_down = gaussian(arg_keys[5], (EXPERTS, D, FF), D ** -0.5, 0.1875, ((0, 16), (1, 2)))
    dir_gate = gaussian(arg_keys[6], (EXPERTS, D, FF), D ** -0.5, 0.1875, ((0, 16), (1, 2)))
    return {"tokens": tokens, "query": query, "expert_ids": expert_ids, "gate_probs": gate_probs, "w_gate_up": w_gate_up, "w_down": w_down, "dir_gate": dir_gate}


def expert_term(token_rows, query_rows, gate_rows, gate_up, down_rows, direction):
    scaled = (gate_rows[:, None].astype(jnp.float32) * query_rows.astype(jnp.float32)).astype(jnp.bfloat16)
    pre_act = jnp.dot(token_rows, gate_up, preferred_element_type=jnp.float32)
    gate_pre = pre_act[:, :FF]
    up_pre = pre_act[:, FF:]
    tangent = jnp.dot(token_rows, direction, preferred_element_type=jnp.float32)
    error_hidden = jnp.dot(scaled, down_rows, preferred_element_type=jnp.float32)
    sigmoid_a = 1.0 / (1.0 + jnp.exp(-gate_pre))
    slope = sigmoid_a * (1.0 + gate_pre * (1.0 - sigmoid_a))
    bend = sigmoid_a * (1.0 - sigmoid_a) * (2.0 + gate_pre * (1.0 - 2.0 * sigmoid_a))
    factors = jnp.concatenate([error_hidden * up_pre * bend * tangent, error_hidden * slope * tangent], axis=1).astype(jnp.bfloat16)
    return jnp.dot(token_rows.T, factors, preferred_element_type=jnp.float32)


def reference(tokens, query, expert_ids, gate_probs, w_gate_up, w_down, dir_gate):
    group_tokens = tokens.reshape(N_REP, TOK_REP, D)
    group_query = query.reshape(N_REP, TOK_REP, D)
    group_ids = expert_ids.reshape(N_REP, TOK_REP, TOPK)
    group_gates = gate_probs.reshape(N_REP, TOK_REP, TOPK)
    limit = N_EP * CAP

    def per_expert(inputs):
        expert, gate_up, down_rows, direction = inputs

        def per_group(group):
            token_block, query_block, id_block, gate_block = group
            routed = id_block == expert
            gate_sum = jnp.sum(jnp.where(routed, gate_block.astype(jnp.float32), jnp.float32(0.0)), axis=1)
            any_routed = jnp.any(routed, axis=1)
            picked = jnp.nonzero(any_routed, size=limit, fill_value=0)[0].astype(jnp.int32)
            total = jnp.sum(any_routed.astype(jnp.int32))
            is_real = jnp.arange(limit, dtype=jnp.int32) < total
            gate_rows = jnp.where(is_real, gate_sum[picked], jnp.float32(0.0)).astype(jnp.bfloat16)
            term = expert_term(token_block[picked], query_block[picked], gate_rows, gate_up, down_rows, direction)
            return term.astype(jnp.bfloat16)

        partials = lax.map(per_group, (group_tokens, group_query, group_ids, group_gates))
        return jnp.sum(partials.astype(jnp.float32), axis=0)

    numbers = jnp.arange(EXPERTS, dtype=jnp.int32)
    return lax.map(per_expert, (numbers, w_gate_up, w_down, dir_gate))
```

```python
import jax
import jax.numpy as jnp
from jax import lax
from jax.sharding import PartitionSpec as P


def make_factors(gate_pre, up_pre, error_hidden, tangent):
    sigmoid_a = 1.0 / (1.0 + jnp.exp(-gate_pre))
    slope = sigmoid_a * (1.0 + gate_pre * (1.0 - sigmoid_a))
    bend = sigmoid_a * (1.0 - sigmoid_a) * (2.0 + gate_pre * (1.0 - 2.0 * sigmoid_a))
    common = error_hidden * tangent
    return (common * up_pre * bend).astype(jnp.bfloat16), (common * slope).astype(jnp.bfloat16)


def dot(a, b, contract=((1,), (0,))):
    return lax.dot_general(a, b, (contract, ((), ())), preferred_element_type=jnp.float32)


def on_device(tokens, query, expert_ids, gate_probs, w_gate_up, w_down, dir_gate):
    experts = lax.axis_size("ep")
    reps = lax.axis_size("rep")
    me = lax.axis_index("ep")
    tok_count, top_count = expert_ids.shape
    model_width = tokens.shape[1]
    hidden_width = dir_gate.shape[2]
    capacity = tok_count * top_count // experts + 1
    capacity = -(-capacity // 16) * 16

    if reps == 2:
        pairs = [(0, 1), (1, 0)]
        w_down_far = lax.ppermute(w_down[0], "rep", pairs)
        dir_far = lax.ppermute(dir_gate[0], "rep", pairs)

    meta = jnp.concatenate([expert_ids.astype(jnp.bfloat16), gate_probs], axis=1).T
    meta = lax.all_gather(meta, "ep", axis=0, tiled=False)
    all_tokens = lax.all_gather(tokens, "ep", axis=0, tiled=False)
    all_query = lax.all_gather(query, "ep", axis=0, tiled=False)

    routed = (meta[:, :top_count].astype(jnp.int32) == me).astype(jnp.float32)
    gates = jnp.sum(routed * meta[:, top_count:].astype(jnp.float32), axis=1)
    chosen = jnp.sum(routed, axis=1)
    order = jnp.arange(tok_count, dtype=jnp.int32)
    before = (order[:, None] < order[None, :]).astype(jnp.bfloat16)
    rank = dot(chosen.astype(jnp.bfloat16), before)
    slots = jnp.arange(capacity, dtype=jnp.float32)
    match = (rank[:, None, :] == slots[None, :, None]) & (chosen[:, None, :] > 0.5)
    place = match.astype(jnp.bfloat16)
    gate_rows = jnp.sum(jnp.where(match, gates[:, None, :], 0.0), axis=2)

    def pick(rows):
        return lax.dot_general(
            place, rows, (((2,), (1,)), ((0,), (0,))), preferred_element_type=jnp.float32
        )

    token_rows = pick(all_tokens).astype(jnp.bfloat16).reshape(-1, model_width)
    scaled = (gate_rows[:, :, None] * pick(all_query)).astype(jnp.bfloat16).reshape(-1, model_width)

    pre_act = dot(token_rows, w_gate_up[0])
    if reps == 2:
        half = model_width // 2
        own_at = lax.axis_index("rep") * half
        far_at = half - own_at

        def columns(array, at):
            return lax.dynamic_slice_in_dim(array, at, half, axis=1)

        near_tokens, far_tokens = columns(token_rows, own_at), columns(token_rows, far_at)
        error = dot(columns(scaled, own_at), w_down[0]) + dot(columns(scaled, far_at), w_down_far)
        tangent = dot(near_tokens, dir_gate[0]) + dot(far_tokens, dir_far)
        parts = make_factors(
            pre_act[:, :hidden_width], pre_act[:, hidden_width:], error, tangent
        )
        first = ((0,), (0,))
        got = [
            lax.ppermute(dot(far_tokens, part, first).astype(jnp.bfloat16), "rep", pairs)
            for part in parts
        ]
        kept = [dot(near_tokens, part, first) for part in parts]
        return jnp.concatenate(
            [k + g.astype(jnp.float32) for k, g in zip(kept, got)], axis=1
        )[None]
    error = dot(scaled, lax.all_gather(w_down[0], "rep", axis=0, tiled=True))
    tangent = dot(token_rows, lax.all_gather(dir_gate[0], "rep", axis=0, tiled=True))
    factors = jnp.concatenate(
        make_factors(pre_act[:, :hidden_width], pre_act[:, hidden_width:], error, tangent), axis=1
    )
    own_rows = lax.psum_scatter(
        dot(token_rows, factors, ((0,), (0,))).astype(jnp.bfloat16),
        "rep",
        scatter_dimension=0,
        tiled=True,
    ).astype(jnp.float32)
    return own_rows[None]


def solution(mesh):
    return jax.shard_map(
        on_device,
        mesh=mesh,
        in_specs=(
            P(("rep", "ep"), None),
            P(("rep", "ep"), None),
            P(("rep", "ep"), None),
            P(("rep", "ep"), None),
            P("ep", None, None),
            P("ep", "rep", None),
            P("ep", "rep", None),
        ),
        out_specs=P("ep", "rep", None),
        check_vma=False,
    )
```

```python
import jax
import jax.numpy as jnp
from jax import lax
from jax.sharding import PartitionSpec as P


def make_factors(gate_pre, up_pre, error_hidden, tangent):
    sigmoid_a = 1.0 / (1.0 + jnp.exp(-gate_pre))
    slope = sigmoid_a * (1.0 + gate_pre * (1.0 - sigmoid_a))
    bend = sigmoid_a * (1.0 - sigmoid_a) * (2.0 + gate_pre * (1.0 - 2.0 * sigmoid_a))
    common = error_hidden * tangent
    return (common * up_pre * bend).astype(jnp.bfloat16), (common * slope).astype(jnp.bfloat16)


def dot(a, b, contract=((1,), (0,))):
    return lax.dot_general(a, b, (contract, ((), ())), preferred_element_type=jnp.float32)


def on_device(tokens, query, expert_ids, gate_probs, w_gate_up, w_down, dir_gate):
    experts = lax.axis_size("ep")
    reps = lax.axis_size("rep")
    me = lax.axis_index("ep")
    tok_count, top_count = expert_ids.shape
    model_width = tokens.shape[1]
    hidden_width = dir_gate.shape[2]
    capacity = tok_count * top_count // experts + 1
    capacity = -(-capacity // 16) * 16

    if reps == 2:
        pairs = [(0, 1), (1, 0)]
        w_down_far = lax.ppermute(w_down[0], "rep", pairs)
        dir_far = lax.ppermute(dir_gate[0], "rep", pairs)

    meta = jnp.concatenate([expert_ids.astype(jnp.bfloat16), gate_probs], axis=1).T

    order = jnp.arange(tok_count, dtype=jnp.int32)
    before = (order[:, None] < order[None, :]).astype(jnp.bfloat16)
    slots = jnp.arange(capacity, dtype=jnp.float32)

    def pick(all_tokens, all_query, meta):
        routed = (meta[:, :top_count].astype(jnp.int32) == me).astype(jnp.float32)
        gates = jnp.sum(
            routed * meta[:, top_count : 2 * top_count].astype(jnp.float32), axis=1
        )
        chosen = jnp.sum(routed, axis=1)
        rank = dot(chosen.astype(jnp.bfloat16), before)
        match = (rank[:, None, :] == slots[None, :, None]) & (chosen[:, None, :] > 0.5)
        place = match.astype(jnp.bfloat16)
        gate_rows = jnp.sum(jnp.where(match, gates[:, None, :], 0.0), axis=2)
        picked = [
            lax.dot_general(
                place, rows, (((2,), (1,)), ((0,), (0,))), preferred_element_type=jnp.float32
            )
            for rows in (all_tokens, all_query)
        ]
        token_rows = picked[0].astype(jnp.bfloat16).reshape(-1, model_width)
        scaled = (gate_rows[:, :, None] * picked[1]).astype(jnp.bfloat16)
        return token_rows, scaled.reshape(-1, model_width)

    def split(blocks):
        return (
            blocks[:, :tok_count],
            blocks[:, tok_count : 2 * tok_count],
            blocks[:, 2 * tok_count :, :tok_count],
        )

    if experts == 16 and reps == 2:
        meta_rows = -(-2 * top_count // 16) * 16
        meta = jnp.pad(meta, ((0, meta_rows - 2 * top_count), (0, model_width - tok_count)))
        block = jnp.concatenate([tokens, query, meta], axis=0)

        def move(array, target):
            return lax.ppermute(array, "ep", [(i, target(i)) for i in range(experts)])

        lane = [block] + [move(block, lambda i: (i + 4 * k) % experts) for k in (1, 3, 2)]
        across = [move(each, lambda i: i ^ 2) for each in lane]
        near, far = jnp.stack(lane), jnp.stack(across)
        groups = [
            [split(near), split(move(near, lambda i: i ^ 1))],
            [split(far), split(move(far, lambda i: i ^ 1))],
        ]
    else:
        groups = [
            [[lax.all_gather(each, "ep", axis=0, tiled=False) for each in (tokens, query, meta)]]
        ]
    rows = []
    for group in groups:
        picked = [pick(*blocks) for blocks in group]
        rows.append([jnp.concatenate(part, axis=0) for part in zip(*picked)])

    if reps == 2:
        half = model_width // 2
        own_at = lax.axis_index("rep") * half
        far_at = half - own_at

        def columns(array, at):
            return lax.dynamic_slice_in_dim(array, at, half, axis=1)

        near_tokens, far_tokens, factors = [], [], []
        for token_rows, scaled in rows:
            pre_act = dot(token_rows, w_gate_up[0])
            near_tokens.append(columns(token_rows, own_at))
            far_tokens.append(columns(token_rows, far_at))
            error = dot(columns(scaled, own_at), w_down[0]) + dot(
                columns(scaled, far_at), w_down_far
            )
            tangent = dot(near_tokens[-1], dir_gate[0]) + dot(far_tokens[-1], dir_far)
            factors.append(
                make_factors(pre_act[:, :hidden_width], pre_act[:, hidden_width:], error, tangent)
            )
        near_tokens, far_tokens = jnp.concatenate(near_tokens), jnp.concatenate(far_tokens)
        parts = [jnp.concatenate(part) for part in zip(*factors)]
        first = ((0,), (0,))
        got = [
            lax.ppermute(dot(far_tokens, part, first).astype(jnp.bfloat16), "rep", pairs)
            for part in parts
        ]
        kept = [dot(near_tokens, part, first) for part in parts]
        return jnp.concatenate(
            [k + g.astype(jnp.float32) for k, g in zip(kept, got)], axis=1
        )[None]
    token_rows, scaled = rows[0]
    pre_act = dot(token_rows, w_gate_up[0])
    error = dot(scaled, lax.all_gather(w_down[0], "rep", axis=0, tiled=True))
    tangent = dot(token_rows, lax.all_gather(dir_gate[0], "rep", axis=0, tiled=True))
    factors = jnp.concatenate(
        make_factors(pre_act[:, :hidden_width], pre_act[:, hidden_width:], error, tangent), axis=1
    )
    own_rows = lax.psum_scatter(
        dot(token_rows, factors, ((0,), (0,))).astype(jnp.bfloat16),
        "rep",
        scatter_dimension=0,
        tiled=True,
    ).astype(jnp.float32)
    return own_rows[None]


def solution(mesh):
    return jax.shard_map(
        on_device,
        mesh=mesh,
        in_specs=(
            P(("rep", "ep"), None),
            P(("rep", "ep"), None),
            P(("rep", "ep"), None),
            P(("rep", "ep"), None),
            P("ep", None, None),
            P("ep", "rep", None),
            P("ep", "rep", None),
        ),
        out_specs=P("ep", "rep", None),
        check_vma=False,
    )
```

```python
import jax
import jax.numpy as jnp
from jax import lax
from jax.sharding import PartitionSpec as P


def make_factors(gate_pre, up_pre, error_hidden, tangent):
    sigmoid_a = 1.0 / (1.0 + jnp.exp(-gate_pre))
    slope = sigmoid_a * (1.0 + gate_pre * (1.0 - sigmoid_a))
    bend = sigmoid_a * (1.0 - sigmoid_a) * (2.0 + gate_pre * (1.0 - 2.0 * sigmoid_a))
    common = error_hidden * tangent
    return (common * up_pre * bend).astype(jnp.bfloat16), (common * slope).astype(jnp.bfloat16)


def dot(a, b, contract=((1,), (0,))):
    return lax.dot_general(a, b, (contract, ((), ())), preferred_element_type=jnp.float32)


def on_device(tokens, query, expert_ids, gate_probs, w_gate_up, w_down, dir_gate):
    experts = lax.axis_size("ep")
    reps = lax.axis_size("rep")
    me = lax.axis_index("ep")
    tok_count, top_count = expert_ids.shape
    model_width = tokens.shape[1]
    hidden_width = dir_gate.shape[2]
    capacity = tok_count * top_count // experts + 1
    capacity = -(-capacity // 16) * 16

    if reps == 2:
        pairs = [(0, 1), (1, 0)]
        w_down_far = lax.ppermute(w_down[0], "rep", pairs)
        dir_far = lax.ppermute(dir_gate[0], "rep", pairs)

    meta = jnp.concatenate([expert_ids.astype(jnp.bfloat16), gate_probs], axis=1).T

    order = jnp.arange(tok_count, dtype=jnp.int32)
    before = (order[:, None] < order[None, :]).astype(jnp.bfloat16)
    slots = jnp.arange(capacity, dtype=jnp.float32)

    def pick(all_tokens, all_query, meta):
        routed = (meta[:, :top_count].astype(jnp.int32) == me).astype(jnp.float32)
        gates = jnp.sum(
            routed * meta[:, top_count : 2 * top_count].astype(jnp.float32), axis=1
        )
        chosen = jnp.sum(routed, axis=1)
        rank = dot(chosen.astype(jnp.bfloat16), before)
        match = (rank[:, None, :] == slots[None, :, None]) & (chosen[:, None, :] > 0.5)
        place = match.astype(jnp.bfloat16)
        gate_rows = jnp.sum(jnp.where(match, gates[:, None, :], 0.0), axis=2)
        picked = [
            lax.dot_general(
                place, rows, (((2,), (1,)), ((0,), (0,))), preferred_element_type=jnp.float32
            )
            for rows in (all_tokens, all_query)
        ]
        token_rows = picked[0].astype(jnp.bfloat16).reshape(-1, model_width)
        scaled = (gate_rows[:, :, None] * picked[1]).astype(jnp.bfloat16)
        return token_rows, scaled.reshape(-1, model_width)

    def split(blocks):
        return (
            blocks[:, :tok_count],
            blocks[:, tok_count : 2 * tok_count],
            blocks[:, 2 * tok_count :, :tok_count],
        )

    if experts == 16 and reps == 2:
        meta_rows = -(-2 * top_count // 16) * 16
        meta = jnp.pad(meta, ((0, meta_rows - 2 * top_count), (0, model_width - tok_count)))
        block = jnp.concatenate([tokens, query, meta], axis=0)

        def move(array, target):
            return lax.ppermute(array, "ep", [(i, target(i)) for i in range(experts)])

        lane, across = [block], [move(block, lambda i: i ^ 2)]
        for k in (1, 3, 2):
            sent = block if k == 1 else block + lane[-1][-1:, -1:]
            lane.append(move(sent, lambda i: (i + 4 * k) % experts))
            across.append(move(lane[-1], lambda i: i ^ 2))
        near, far = jnp.stack(lane), jnp.stack(across)
        groups = [
            [split(near), split(move(near, lambda i: i ^ 1))],
            [split(far), split(move(far, lambda i: i ^ 1))],
        ]
    else:
        groups = [
            [[lax.all_gather(each, "ep", axis=0, tiled=False) for each in (tokens, query, meta)]]
        ]
    rows = []
    for group in groups:
        picked = [pick(*blocks) for blocks in group]
        rows.append([jnp.concatenate(part, axis=0) for part in zip(*picked)])

    if reps == 2:
        half = model_width // 2
        own_at = lax.axis_index("rep") * half
        far_at = half - own_at

        def columns(array, at):
            return lax.dynamic_slice_in_dim(array, at, half, axis=1)

        near_tokens, far_tokens, factors = [], [], []
        for token_rows, scaled in rows:
            pre_act = dot(token_rows, w_gate_up[0])
            near_tokens.append(columns(token_rows, own_at))
            far_tokens.append(columns(token_rows, far_at))
            error = dot(columns(scaled, own_at), w_down[0]) + dot(
                columns(scaled, far_at), w_down_far
            )
            tangent = dot(near_tokens[-1], dir_gate[0]) + dot(far_tokens[-1], dir_far)
            factors.append(
                make_factors(pre_act[:, :hidden_width], pre_act[:, hidden_width:], error, tangent)
            )
        near_tokens, far_tokens = jnp.concatenate(near_tokens), jnp.concatenate(far_tokens)
        parts = [jnp.concatenate(part) for part in zip(*factors)]
        first = ((0,), (0,))
        got = [
            lax.ppermute(dot(far_tokens, part, first).astype(jnp.bfloat16), "rep", pairs)
            for part in parts
        ]
        kept = [dot(near_tokens, part, first) for part in parts]
        return jnp.concatenate(
            [k + g.astype(jnp.float32) for k, g in zip(kept, got)], axis=1
        )[None]
    token_rows, scaled = rows[0]
    pre_act = dot(token_rows, w_gate_up[0])
    error = dot(scaled, lax.all_gather(w_down[0], "rep", axis=0, tiled=True))
    tangent = dot(token_rows, lax.all_gather(dir_gate[0], "rep", axis=0, tiled=True))
    factors = jnp.concatenate(
        make_factors(pre_act[:, :hidden_width], pre_act[:, hidden_width:], error, tangent), axis=1
    )
    own_rows = lax.psum_scatter(
        dot(token_rows, factors, ((0,), (0,))).astype(jnp.bfloat16),
        "rep",
        scatter_dimension=0,
        tiled=True,
    ).astype(jnp.float32)
    return own_rows[None]


def solution(mesh):
    return jax.shard_map(
        on_device,
        mesh=mesh,
        in_specs=(
            P(("rep", "ep"), None),
            P(("rep", "ep"), None),
            P(("rep", "ep"), None),
            P(("rep", "ep"), None),
            P("ep", None, None),
            P("ep", "rep", None),
            P("ep", "rep", None),
        ),
        out_specs=P("ep", "rep", None),
        check_vma=False,
    )
```
